512 devices in a mesh: table: 64 (over z, y), rep: 8 (over x, core).
Axes of the slice: x: 4, y: 8, z: 8, core: 2. Of those that a mesh axis runs over, the one named last changes fastest.
Arguments:
- bag_rows: int32 [512, 1024, 8], P(('table', 'rep')), may hold values from 0 to 2047
- bag_owner: int32 [512, 1024, 8], P(('table', 'rep')), may hold values from 0 to 63, all different within a row; in each aligned block of 1024 rows (0 to 1023, 1024 to 2047, ..., all dimensions but the last counted through in order) at most 192 rows name the same one
- bag_weight: float32 [512, 1024, 8], P(('table', 'rep')), may hold values from 0.25 to 2
- tables: bfloat16 [4, 131072, 128], P(None, 'table'), may hold values from -3 to 3
- returning: int32 [512], P(('table', 'rep')), may hold values 0 or 1
- home: int32 [512], P(('table', 'rep')), may hold values from 0 to 7
- entry: int32 [512], P(('table', 'rep')), may hold values from 0 to 7
- stores: bfloat16 [4096, 30, 512], P(('table', 'rep')), may hold values from -6 to 6
- conv_weight: bfloat16 [4, 1536, 512], P(None, 'table'), may hold values from -0.15625 to 0.15625
- norm_gain: float32 [4, 512], replicated, may hold values from 0.1 to 1.9
Outputs:
- hidden: bfloat16 [512, 1024, 512], P(('table', 'rep'))
The draws below stay inside these ranges and needn't reach their ends.
Inputs may be any that keep to these rules, and one draw needn't show every extreme that they name: `bag_owner`: the 8 ids of one slot name different owners. Among the slots of one device no owner is named by more than 192 ids, and in some devices' slots one owner is named by exactly 192.
All inputs are finite; a program needn't handle non-finite values. No bound on the sum of `returning` on one device may be relied on, other than what follows from the above.
Results may differ from the reference program's by a relative error of at most 0.0057.
Values may be sent and summed in bfloat16 or wider, within the bound.
A program may use at most 64 MiB of HBM per device.

```python
import math
import jax
import jax.numpy as jnp
import numpy as np
from jax import lax

E = 128
NTAB = 4
C = 512
BAGTOT = 8
SLOTS = 1024
SAMP_DEV = 1
LAYERS = 4
ROWS_DEV = 2048
STORE_DEV = 8
STATE_LEN = 30
TOK_DEV = 1024
SAMPLES = 512
ROWS = 131072
STORED = 4096
CAP = 192
N_TABLE = 64
N_REP = 8


def set_ends(entries, stream_key, smallest, top_value):
    longest = entries.shape.index(max(entries.shape))
    spots = []
    for shift in (0, 1):
        where = [jax.random.randint(jax.random.fold_in(stream_key, axis), (), 0, length) for axis, length in enumerate(entries.shape)]
        where[longest] = (where[longest] + shift) % entries.shape[longest]
        spots.append(tuple(where))
    return entries.at[spots[0]].set(smallest).at[spots[1]].set(top_value)


def level_of(key, extent, shards, smallest, high):
    def one(position, shards_of):
        steps = jax.random.uniform(jax.random.fold_in(jax.random.fold_in(key, 6), position), (shards_of,), jnp.float32, smallest / len(shards), high / len(shards))
        return jnp.repeat(jnp.exp(steps), extent[position] // shards_of).reshape((-1,) + (1,) * (len(extent) - position - 1))

    level = one(*shards[0])
    for cut in shards[1:]:
        level = level * one(*cut)
    return level


def deal_out(key, own, number, rows, count, top, reach, skew):
    ranking = jax.random.permutation(key, count)
    crowded, common = shares(count, rows * top, reach, skew, True), shares(count, rows * top, reach, skew, False)
    places = jnp.arange(count)

    def named(tallies, rotation):
        used = int((tallies > 0).sum())
        fixed = max(1, used // 4)
        moved = fixed + (places - fixed + rotation * (used - fixed)) % max(1, count - fixed)
        return jnp.zeros((count,), jnp.int32).at[ranking[jnp.where(places < fixed, places, moved)]].set(jnp.asarray(tallies, jnp.int32))

    tallies = jnp.where(number % 4 == 0, named(crowded, number // 4), named(common, number - number // 4 - 1))
    mixed = jax.random.permutation(jax.random.fold_in(own, 3), count)
    giver, taker = mixed[0:count // 2 * 2:2], mixed[1:count // 2 * 2:2]
    room = jnp.minimum(tallies[giver] - 1, reach - tallies[taker]) // 2
    room = jnp.where((giver == ranking[0]) | (taker == ranking[0]) | (tallies[taker] == 0), 0, jnp.maximum(room, 0))
    moved = jax.random.randint(jax.random.fold_in(own, 4), (count // 2,), 0, 1 << 20) % (room + 1)
    tallies = tallies.at[giver].add(-moved).at[taker].add(moved)
    items = jnp.searchsorted(jnp.cumsum(tallies), jnp.arange(rows * top), side="right").astype(jnp.int32)
    table = items.reshape(top, rows).T
    table = table[jax.random.permutation(jax.random.fold_in(own, 1), rows)]
    rotation = jax.random.randint(jax.random.fold_in(own, 2), (rows, 1), 0, top)
    return jnp.take_along_axis(table, (jnp.arange(top)[None, :] + rotation) % top, axis=1)


def shares(amount, total, most, lean, full):
    loads = [(1 << 20) // math.isqrt(rank ** lean) + 1 for rank in range(1, amount + 1)]
    largest = most if full else min(most, max(-(-total // amount), total * loads[0] // sum(loads)))
    least = 1 if total - largest >= amount - 1 else 0
    given, spare = [largest] + [least] * (amount - 1), total - largest - least * (amount - 1)
    while spare > 0:
        movable = [i for i in range(1, amount) if given[i] < largest] or [i for i in range(1, amount) if given[i] < most]
        mass, left = sum([loads[i] for i in movable]), spare
        for i in movable:
            more = min(most - given[i], max(1, left * loads[i] // mass), spare)
            given[i] = given[i] + more
            spare = spare - more
    return np.array(given)


def normal_values(own_key, dims, scale, limit, shards=(), kind=jnp.bfloat16):
    drawn = scale * jax.random.normal(own_key, dims, jnp.float32)
    if shards:
        drawn = drawn * level_of(own_key, dims, shards, -0.22, 0.18)
    return jnp.clip(drawn, -limit, limit).astype(kind)


def setup_inputs(seed: int = 0) -> dict:
    key_of = jax.random.split(jax.random.key(seed), 11)
    bag_rows = set_ends(jax.random.randint(key_of[0], (SAMPLES, SLOTS, BAGTOT), 0, ROWS_DEV), jax.random.fold_in(key_of[0], 1), 0, ROWS_DEV - 1).astype(jnp.int32)
    bag_owner_keys = jax.random.split(jax.random.fold_in(key_of[1], 1), SAMPLES * SLOTS // TOK_DEV)
    bag_owner_turns = jax.random.permutation(jax.random.fold_in(key_of[1], 3), SAMPLES * SLOTS // TOK_DEV)
    bag_owner = jax.vmap(lambda own, number: deal_out(jax.random.fold_in(key_of[1], 2), own, number, TOK_DEV, N_TABLE, BAGTOT, CAP, 2))(bag_owner_keys, bag_owner_turns).reshape((SAMPLES, SLOTS, BAGTOT))
    bag_weight = jnp.clip(jnp.exp(math.log(2.0) - 2.0794415 * jax.random.uniform(key_of[2], (SAMPLES, SLOTS, BAGTOT), jnp.float32) ** level_of(key_of[2], (SAMPLES, SLOTS, BAGTOT), ((0, 512),), -0.2, 0.2)), 0.25, 2.0)
    tables = normal_values(key_of[3], (NTAB, ROWS, E), 0.5, 3.0, ((1, 64),))
    returning = set_ends((jax.random.randint(key_of[4], (SAMPLES,), 0, 4) < 3).astype(jnp.int32), jax.random.fold_in(key_of[4], 1), 0, 1)
    home = set_ends(jax.random.randint(key_of[5], (SAMPLES,), 0, N_REP), jax.random.fold_in(key_of[5], 1), 0, N_REP - 1).astype(jnp.int32)
    entry = set_ends(jax.random.randint(key_of[6], (SAMPLES,), 0, STORE_DEV), jax.random.fold_in(key_of[6], 1), 0, STORE_DEV - 1).astype(jnp.int32)
    stores = normal_values(key_of[7], (STORED, STATE_LEN, C), 1.0, 6.0, ((0, 512),))
    conv_weight = normal_values(key_of[8], (LAYERS, 3 * C, C), (3 * C) ** -0.5, 0.15625, ((1, 64),))
    norm_gain = jnp.clip(1.0 + 0.18 * jax.random.normal(key_of[9], (LAYERS, C), jnp.float32), 0.1, 1.9)
    return dict(bag_rows=bag_rows, bag_owner=bag_owner, bag_weight=bag_weight, tables=tables, returning=returning, home=home, entry=entry, stores=stores, conv_weight=conv_weight, norm_gain=norm_gain)


table_of_id = (0, 1, 2, 2, 3, 3, 3, 3)
bag_bounds = ((0, 1), (1, 2), (2, 4), (4, 8))
epsilon = 1e-05

def pool_bags(weighted):
    sums = [lax.optimization_barrier(jnp.sum(weighted[..., lower:upper, :], axis=-2)) for lower, upper in bag_bounds]
    return jnp.concatenate(sums, axis=-1)

def norm_relu(values, gain):
    mean = lax.optimization_barrier(jnp.mean(values, axis=-1, keepdims=True))
    centred = values - mean
    spread = lax.optimization_barrier(jnp.mean(centred * centred, axis=-1, keepdims=True))
    return jnp.maximum(centred * lax.rsqrt(spread + epsilon) * gain, 0.0)

def stack_taps(inputs, carried, offset, dilation):
    span = 2 * dilation
    extended = jnp.concatenate([carried[..., offset:offset + span, :], inputs], axis=-2)
    length = inputs.shape[-2]
    taps = [extended[..., span - tap * dilation:span - tap * dilation + length, :] for tap in range(3)]
    return jnp.concatenate(taps, axis=-1)

def reference(bag_rows, bag_owner, bag_weight, tables, returning, home, entry, stores, conv_weight, norm_gain):
    flat_table = tables.reshape(NTAB * ROWS, E)
    table_ids = jnp.array(table_of_id, jnp.int32)
    device_of = jnp.arange(SAMPLES, dtype=jnp.int32) // SAMP_DEV
    store_row = device_of // N_REP * (N_REP * STORE_DEV) + home * STORE_DEV + entry
    carried_all = stores[store_row]
    carried_all = jnp.where(returning[:, None, None] > 0, carried_all, jnp.zeros_like(carried_all))

    def one_sample(item):
        rows, owner, weight, carried = item
        index = table_ids[None, :] * ROWS + owner * ROWS_DEV + rows
        picked = flat_table[index].astype(jnp.float32) * weight[..., None]
        block_in = pool_bags(picked).astype(jnp.bfloat16)
        inputs = block_in
        offset = 0
        for layer in range(LAYERS):
            dilation = 2 ** layer
            stacked = stack_taps(inputs, carried, offset, dilation)
            output = jnp.dot(stacked, conv_weight[layer], preferred_element_type=jnp.float32)
            active = norm_relu(output, norm_gain[layer])
            offset = offset + 2 * dilation
            if layer % 2 == 0:
                inputs = active.astype(jnp.bfloat16)
            else:
                block_in = (active + block_in.astype(jnp.float32)).astype(jnp.bfloat16)
                inputs = block_in
        return block_in
    return lax.map(one_sample, (bag_rows, bag_owner, bag_weight, carried_all))
```

```python
import functools

import jax
import jax.numpy as jnp
from jax import lax
from jax.experimental import pallas as pl
from jax.experimental.pallas import tpu as pltpu
from jax.sharding import PartitionSpec as P

table_of_id = (0, 1, 2, 2, 3, 3, 3, 3)
epsilon = 1e-05
MESH = pl.DeviceIdType.MESH
MIB = 1024 * 1024


def whole(memory=pltpu.VMEM):
    return pl.BlockSpec(memory_space=memory)


def split_index(index):
    return lax.rem(index * 27, 64)


def route_kernel(shard_rows, capacity, owner_ref, rows_ref, req_ref, placed_ref, mem_ref, run_ref):
    slots, bag = owner_ref.shape
    owners = req_ref.shape[0]
    step = 128
    f32, bf16 = jnp.float32, jnp.bfloat16
    lane = lax.broadcasted_iota(jnp.int32, (slots, 128), 1)
    upper = lane >= owners
    lane_owner = jnp.where(upper, lane - owners, lane)
    owned = owner_ref[...]
    local_rows = rows_ref[...]
    named = jnp.zeros((slots, 128), f32)
    for k in range(bag):
        named = named + jnp.where(owned[:, k : k + 1] == lane_owner, 1.0, 0.0)
    mem_ref[...] = named.astype(bf16)
    below = (
        lax.broadcasted_iota(jnp.int32, (step, step), 1)
        < lax.broadcasted_iota(jnp.int32, (step, step), 0)
    ).astype(f32).astype(bf16)
    total = jnp.zeros((1, 128), f32)
    for part in range(slots // step):
        block = mem_ref[part * step : (part + 1) * step, :]
        run_ref[part * step : (part + 1) * step, :] = total + jnp.dot(
            below, block, preferred_element_type=f32
        )
        total = total + jnp.sum(block.astype(f32), axis=0, keepdims=True)
    ranks = run_ref[...]
    spread = (
        (lax.broadcasted_iota(jnp.int32, (128, 256), 0) < owners).astype(f32).astype(bf16)
    )
    column = lax.broadcasted_iota(jnp.int32, (slots, 256), 1).astype(f32)
    pick_row = lax.broadcasted_iota(jnp.int32, (16, 128), 0)
    pick_upper = lax.broadcasted_iota(jnp.int32, (16, 128), 1) >= owners
    requests = jnp.zeros((128, 256), f32)
    places = jnp.zeros((16, slots), f32)
    for k in range(bag):
        hit = owned[:, k : k + 1] == lane_owner
        value = local_rows[:, k : k + 1] + table_of_id[k] * shard_rows
        parts = jnp.where(upper, value & 63, value >> 6)
        words = jnp.where(hit, parts, 0).astype(f32).astype(bf16)
        marks = jnp.where(hit, jnp.where(upper, lane_owner.astype(f32), ranks), 0.0).astype(bf16)
        rank_wide = jnp.dot(marks, spread, preferred_element_type=f32)
        places_here = jnp.where(rank_wide == column, 1.0, 0.0).astype(bf16)
        requests = requests + lax.dot_general(
            words, places_here, (((0,), (0,)), ((), ())), preferred_element_type=f32
        )
        pick = (
            (pick_row == jnp.where(pick_upper, 8 + k, k)).astype(f32).astype(bf16)
        )
        places = places + lax.dot_general(
            pick, marks, (((1,), (1,)), ((), ())), preferred_element_type=f32
        )
    req_ref[...] = (requests[:owners] * 64.0 + requests[owners : 2 * owners]).astype(jnp.int32)
    placed_ref[...] = (places[8:16] * float(capacity) + places[0:8]).astype(jnp.int32)


def exchange_kernel(
    capacity,
    req_ref,
    entry_ref,
    table_ref,
    stores_ref,
    rows_out,
    carried_out,
    wide_table,
    stage,
    send_rows,
    req_in,
    req_words,
    entry_in,
    entry_words,
    send_state,
    req_send,
    req_recv,
    row_send,
    row_recv,
    entry_send,
    entry_recv,
    state_send,
    state_recv,
    local_sem,
):
    owners = req_ref.shape[0]
    peers = entry_in.shape[0]
    side = 8
    me = lax.axis_index("table")
    rep = lax.axis_index("rep")
    my_z, my_y = me // side, lax.rem(me, side)

    def partner(index):
        offset = split_index(index)
        return lax.rem(my_z + offset // side, side) * side + lax.rem(my_y + lax.rem(offset, side), side)

    def origin(index):
        offset = split_index(index)
        return (
            lax.rem(my_z + side - offset // side, side) * side
            + lax.rem(my_y + side - lax.rem(offset, side), side)
        )

    barrier = pltpu.get_barrier_semaphore()

    @pl.loop(1, owners)
    def _(i):
        pl.semaphore_signal(barrier, inc=1, device_id=(partner(i), rep), device_id_type=MESH)

    @pl.loop(1, peers)
    def _(i):
        pl.semaphore_signal(
            barrier, inc=1, device_id=(me, lax.rem(rep + i, peers)), device_id_type=MESH
        )

    pl.semaphore_wait(barrier, owners - 1 + peers - 1)

    def request_copy(index):
        to = partner(index)
        return pltpu.make_async_remote_copy(
            src_ref=req_ref.at[pl.ds(to, 1)],
            dst_ref=req_in.at[pl.ds(me, 1)],
            send_sem=req_send.at[to],
            recv_sem=req_recv.at[me],
            device_id=(to, rep),
            device_id_type=MESH,
        )

    def request_arrival(index):
        source = origin(index)
        return pltpu.make_async_remote_copy(
            src_ref=req_ref.at[pl.ds(source, 1)],
            dst_ref=req_in.at[pl.ds(source, 1)],
            send_sem=req_send.at[source],
            recv_sem=req_recv.at[source],
            device_id=(source, rep),
            device_id_type=MESH,
        )

    def entry_copy(index):
        to = lax.rem(rep + index, peers)
        return pltpu.make_async_remote_copy(
            src_ref=entry_ref,
            dst_ref=entry_in.at[pl.ds(rep, 1)],
            send_sem=entry_send.at[to],
            recv_sem=entry_recv.at[rep],
            device_id=(me, to),
            device_id_type=MESH,
        )

    def entry_arrival(index):
        source = lax.rem(rep + peers - index, peers)
        return pltpu.make_async_remote_copy(
            src_ref=entry_ref,
            dst_ref=entry_in.at[pl.ds(source, 1)],
            send_sem=entry_send.at[source],
            recv_sem=entry_recv.at[source],
            device_id=(me, source),
            device_id_type=MESH,
        )

    def state_copy(index):
        to = lax.rem(rep + index, peers)
        return pltpu.make_async_remote_copy(
            src_ref=send_state.at[to],
            dst_ref=carried_out.at[rep],
            send_sem=state_send.at[to],
            recv_sem=state_recv.at[rep],
            device_id=(me, to),
            device_id_type=MESH,
        )

    def state_arrival(index):
        source = lax.rem(rep + peers - index, peers)
        return pltpu.make_async_remote_copy(
            src_ref=send_state.at[source],
            dst_ref=carried_out.at[source],
            send_sem=state_send.at[source],
            recv_sem=state_recv.at[source],
            device_id=(me, source),
            device_id_type=MESH,
        )

    def row_copy(index):
        to = partner(index)
        return pltpu.make_async_remote_copy(
            src_ref=send_rows.at[to],
            dst_ref=rows_out.at[me],
            send_sem=row_send.at[to],
            recv_sem=row_recv.at[me],
            device_id=(to, rep),
            device_id_type=MESH,
        )

    def row_arrival(index):
        source = origin(index)
        return pltpu.make_async_remote_copy(
            src_ref=send_rows.at[source],
            dst_ref=rows_out.at[source],
            send_sem=row_send.at[source],
            recv_sem=row_recv.at[source],
            device_id=(source, rep),
            device_id_type=MESH,
        )

    @pl.loop(1, owners)
    def _(i):
        request_copy(i).start()

    @pl.loop(1, peers)
    def _(i):
        entry_copy(i).start()

    req_in[pl.ds(me, 1), :] = req_ref[pl.ds(me, 1), :]
    entry_in[pl.ds(rep, 1), :] = entry_ref[...]

    tile = 256

    @pl.loop(0, table_ref.shape[0] // tile)
    def _(i):
        at = pl.multiple_of(i * tile, tile)
        wide_table[pl.ds(at, tile), :] = table_ref[pl.ds(at, tile), :].astype(jnp.float32)

    @pl.loop(1, peers)
    def _(i):
        entry_arrival(i).wait_recv()

    entry_move = pltpu.make_async_copy(entry_in, entry_words, local_sem.at[0])
    entry_move.start()
    entry_move.wait()

    @pl.loop(0, peers)
    def _(i):
        to = lax.rem(rep + i, peers)
        send_state[to] = stores_ref[entry_words[to, 0]]

    @pl.loop(1, peers)
    def _(i):
        state_copy(i).start()

    own_state = pltpu.make_async_copy(send_state.at[rep], carried_out.at[rep], local_sem.at[1])
    own_state.start()

    @pl.loop(1, owners)
    def _(i):
        request_arrival(i).wait_recv()

    req_move = pltpu.make_async_copy(req_in, req_words, local_sem.at[0])
    req_move.start()
    req_move.wait()

    def gather(to):
        @pl.loop(0, capacity // 16)
        def _(c):
            for u in range(16):
                row = req_words[to, c * 16 + u]
                stage[pl.ds(c * 16 + u, 1), :] = wide_table[pl.ds(row, 1), :]

        send_rows[to] = stage[...].astype(jnp.bfloat16)

    @pl.loop(1, owners)
    def _(i):
        gather(partner(i))
        row_copy(i).start()

    gather(me)
    own_rows = pltpu.make_async_copy(send_rows.at[me], rows_out.at[me], local_sem.at[0])
    own_rows.start()
    own_rows.wait()
    own_state.wait()

    @pl.loop(1, owners)
    def _(i):
        request_copy(i).wait_send()

    @pl.loop(1, peers)
    def _(i):
        entry_copy(i).wait_send()
        state_copy(i).wait_send()
        state_arrival(i).wait_recv()

    @pl.loop(1, owners)
    def _(i):
        row_copy(i).wait_send()
        row_arrival(i).wait_recv()


def convolve_kernel(
    rows_ref,
    placed_ref,
    weight_ref,
    where_ref,
    carried_ref,
    filters_ref,
    gain_ref,
    out_ref,
    wide_rows,
    stage,
    even_in,
    odd_in,
):
    f32, bf16 = jnp.float32, jnp.bfloat16
    slots, bag = weight_ref.shape
    width = rows_ref.shape[1]
    channels = out_ref.shape[1]
    layers = filters_ref.shape[0]
    head = even_in.shape[0] - slots
    tile = 512

    @pl.loop(0, rows_ref.shape[0] // tile)
    def _(i):
        at = pl.multiple_of(i * tile, tile)
        wide_rows[pl.ds(at, tile), :] = rows_ref[pl.ds(at, tile), :].astype(f32)

    @pl.loop(0, slots // 8)
    def _(i):
        base = pl.multiple_of(i * 8, 8)
        for k in range(bag):
            for j in range(8):
                stage[k * 8 + j : k * 8 + j + 1, :] = wide_rows[
                    pl.ds(placed_ref[k, base + j], 1), :
                ]
        weights = weight_ref[pl.ds(base, 8), :]
        terms = [stage[k * 8 : k * 8 + 8, :] * weights[:, k : k + 1] for k in range(bag)]
        sums = (
            terms[0],
            terms[1],
            terms[2] + terms[3],
            (terms[4] + terms[5]) + (terms[6] + terms[7]),
        )
        for t in range(4):
            even_in[pl.ds(head + base, 8), t * width : (t + 1) * width] = (
                sums[t].astype(bf16).astype(f32)
            )

    state = carried_ref[where_ref[0]].astype(f32)
    state = jnp.where(where_ref[1] > 0, state, 0.0)
    block = 256
    offset = 0
    for layer in range(layers):
        dilation = 2**layer
        span = 2 * dilation
        source, target = (even_in, odd_in) if layer % 2 == 0 else (odd_in, even_in)
        source[head - span : head, :] = state[offset : offset + span, :]
        offset = offset + span
        for part in range(slots // block):
            low = head + part * block
            taps = [
                source[low - tap * dilation : low - tap * dilation + block, :].astype(bf16)
                for tap in range(3)
            ]
            values = jnp.dot(
                jnp.concatenate(taps, axis=1), filters_ref[layer], preferred_element_type=f32
            )
            mean = jnp.mean(values, axis=-1, keepdims=True)
            centred = values - mean
            spread = jnp.mean(centred * centred, axis=-1, keepdims=True)
            active = jnp.maximum(
                centred * lax.rsqrt(spread + epsilon) * gain_ref[layer : layer + 1, :], 0.0
            )
            if layer % 2 == 1:
                active = active + target[low : low + block, :]
            if layer == layers - 1:
                out_ref[part * block : (part + 1) * block, :] = active.astype(bf16)
            else:
                target[low : low + block, :] = active.astype(bf16).astype(f32)


def local(
    bag_rows, bag_owner, bag_weight, tables, returning, home, entry, stores, conv_weight, norm_gain
):
    i32, f32, bf16 = jnp.int32, jnp.float32, jnp.bfloat16
    owners = lax.axis_size("table")
    peers = lax.axis_size("rep")
    slots, bag = bag_rows.shape[1:]
    shard_rows, width = tables.shape[1:]
    layers, _, channels = conv_weight.shape
    capacity = min(slots, (3 * slots * bag + 2 * owners - 1) // (2 * owners))
    entries, state_len = stores.shape[:2]
    state_rows = 32

    filters = lax.all_gather(conv_weight, "table", axis=1, tiled=True)

    requests, placed = pl.pallas_call(
        functools.partial(route_kernel, shard_rows, capacity),
        out_shape=(
            jax.ShapeDtypeStruct((owners, 256), i32),
            jax.ShapeDtypeStruct((bag, slots), i32),
        ),
        in_specs=[whole(), whole()],
        out_specs=(whole(), whole()),
        scratch_shapes=[pltpu.VMEM((slots, 128), bf16), pltpu.VMEM((slots, 128), f32)],
        compiler_params=pltpu.CompilerParams(vmem_limit_bytes=40 * MIB),
        name="route",
    )(bag_owner[0], bag_rows[0])

    padded = jnp.pad(stores, ((0, 0), (0, state_rows - state_len), (0, 0)))
    rows, carried = pl.pallas_call(
        functools.partial(exchange_kernel, capacity),
        out_shape=(
            jax.ShapeDtypeStruct((owners, capacity, width), bf16),
            jax.ShapeDtypeStruct((peers, state_rows, channels), bf16),
        ),
        in_specs=[whole(), whole(), whole(), whole()],
        out_specs=(whole(pl.ANY), whole(pl.ANY)),
        scratch_shapes=[
            pltpu.VMEM((4 * shard_rows, width), f32),
            pltpu.VMEM((capacity, width), f32),
            pltpu.VMEM((owners, capacity, width), bf16),
            pltpu.VMEM((owners, 256), i32),
            pltpu.SMEM((owners, 256), i32),
            pltpu.VMEM((peers, 128), i32),
            pltpu.SMEM((peers, 128), i32),
            pltpu.VMEM((peers, state_rows, channels), bf16),
            pltpu.SemaphoreType.DMA((owners,)),
            pltpu.SemaphoreType.DMA((owners,)),
            pltpu.SemaphoreType.DMA((owners,)),
            pltpu.SemaphoreType.DMA((owners,)),
            pltpu.SemaphoreType.DMA((peers,)),
            pltpu.SemaphoreType.DMA((peers,)),
            pltpu.SemaphoreType.DMA((peers,)),
            pltpu.SemaphoreType.DMA((peers,)),
            pltpu.SemaphoreType.DMA((2,)),
        ],
        compiler_params=pltpu.CompilerParams(
            collective_id=0, has_side_effects=True, vmem_limit_bytes=40 * MIB
        ),
        name="exchange",
    )(
        requests,
        jnp.broadcast_to(entry[:, None], (1, 128)),
        tables.reshape(4 * shard_rows, width),
        padded,
    )

    hidden = pl.pallas_call(
        convolve_kernel,
        out_shape=jax.ShapeDtypeStruct((slots, channels), bf16),
        in_specs=[
            whole(),
            whole(pltpu.SMEM),
            whole(),
            whole(pltpu.SMEM),
            whole(),
            whole(),
            whole(),
        ],
        out_specs=whole(),
        scratch_shapes=[
            pltpu.VMEM((owners * capacity, width), f32),
            pltpu.VMEM((8 * bag, width), f32),
            pltpu.VMEM((32 + slots, channels), f32),
            pltpu.VMEM((32 + slots, channels), f32),
        ],
        compiler_params=pltpu.CompilerParams(vmem_limit_bytes=48 * MIB),
        name="convolve",
    )(
        rows.reshape(owners * capacity, width),
        placed,
        bag_weight[0],
        jnp.concatenate([home, returning]),
        carried,
        filters,
        norm_gain,
    )
    return hidden[None]


def solution(mesh):
    in_specs = (
        P(("table", "rep"), None, None),
        P(("table", "rep"), None, None),
        P(("table", "rep"), None, None),
        P(None, "table", None),
        P(("table", "rep")),
        P(("table", "rep")),
        P(("table", "rep")),
        P(("table", "rep"), None, None),
        P(None, "table", None),
        P(),
    )
    out_specs = P(("table", "rep"), None, None)
    return jax.shard_map(local, mesh=mesh, in_specs=in_specs, out_specs=out_specs, check_vma=False)
```

```python
import functools

import jax
import jax.numpy as jnp
from jax import lax
from jax.experimental import pallas as pl
from jax.experimental.pallas import tpu as pltpu
from jax.sharding import PartitionSpec as P

table_of_id = (0, 1, 2, 2, 3, 3, 3, 3)
epsilon = 1e-05
MESH = pl.DeviceIdType.MESH
MIB = 1024 * 1024


def whole(memory=pltpu.VMEM):
    return pl.BlockSpec(memory_space=memory)


def split_index(index):
    return lax.rem(index * 27, 64)


def route(shard_rows, capacity, owner_ref, rows_ref, req_ref, placed_ref):
    bag, slots = owner_ref.shape
    owners, columns = req_ref.shape
    step = 256
    f32, bf16 = jnp.float32, jnp.bfloat16
    owner_row = lax.broadcasted_iota(jnp.int32, (owners, slots), 0)
    named = jnp.zeros((owners, slots), f32)
    for k in range(bag):
        named = named + jnp.where(owner_ref[k : k + 1, :] == owner_row, 1.0, 0.0)
    before = (
        lax.broadcasted_iota(jnp.int32, (step, step), 0)
        < lax.broadcasted_iota(jnp.int32, (step, step), 1)
    ).astype(f32).astype(bf16)
    total = jnp.zeros((owners, 1), f32)
    ranked = []
    for part in range(slots // step):
        block = named[:, part * step : (part + 1) * step]
        ranked.append(total + jnp.dot(block.astype(bf16), before, preferred_element_type=f32))
        total = total + jnp.sum(block, axis=1, keepdims=True)
    ranks = jnp.concatenate(ranked, axis=1)
    place_row = lax.broadcasted_iota(jnp.int32, (columns, slots), 0)
    requests = jnp.zeros((2 * owners, columns), f32)
    for k in range(bag):
        owner = owner_ref[k : k + 1, :]
        hit = owner == owner_row
        rank = jnp.sum(jnp.where(hit, ranks, 0.0), axis=0, keepdims=True).astype(jnp.int32)
        placed_ref[k : k + 1, :] = owner * capacity + rank
        value = rows_ref[k : k + 1, :] + table_of_id[k] * shard_rows
        high = jnp.where(hit, (value >> 6).astype(f32), 0.0)
        low = jnp.where(hit, (value & 63).astype(f32), 0.0)
        words = jnp.concatenate([high, low], axis=0).astype(bf16)
        marks = jnp.where(place_row == rank, 1.0, 0.0).astype(bf16)
        requests = requests + lax.dot_general(
            words, marks, (((1,), (1,)), ((), ())), preferred_element_type=f32
        )
    wanted = (requests[:owners] * 64.0 + requests[owners:]).astype(jnp.int32)
    req_ref[...] = jnp.clip(wanted, 0, 4 * shard_rows - 1)


def exchange_kernel(
    shard_rows,
    capacity,
    owner_ref,
    bag_rows_ref,
    entry_ref,
    table_ref,
    stores_ref,
    shard_ref,
    placed_out,
    rows_out,
    carried_out,
    filters_out,
    table_here,
    stores_here,
    wide_table,
    wide_stores,
    state_stage,
    stage,
    send_rows,
    req_ref,
    req_in,
    req_words,
    entry_in,
    entry_words,
    send_state,
    pieces,
    gathered,
    req_send,
    req_recv,
    row_send,
    row_recv,
    entry_send,
    entry_recv,
    state_send,
    state_recv,
    near_send,
    near_recv,
    far_send,
    far_recv,
    line_send,
    line_recv,
    core_send,
    core_recv,
    local_sem,
):
    owners = req_ref.shape[0]
    peers = entry_in.shape[0]
    side = 8
    me = lax.axis_index("table")
    rep = lax.axis_index("rep")
    my_z, my_y = me // side, lax.rem(me, side)

    def partner(index):
        offset = split_index(index)
        return lax.rem(my_z + offset // side, side) * side + lax.rem(my_y + lax.rem(offset, side), side)

    def origin(index):
        offset = split_index(index)
        return (
            lax.rem(my_z + side - offset // side, side) * side
            + lax.rem(my_y + side - lax.rem(offset, side), side)
        )

    def remote(source, target, sender, receiver, table, line):
        return pltpu.make_async_remote_copy(
            src_ref=source,
            dst_ref=target,
            send_sem=sender,
            recv_sem=receiver,
            device_id=(table, line),
            device_id_type=MESH,
        )

    def request_copy(index):
        to = partner(index)
        return remote(
            req_ref.at[pl.ds(to, 1)], req_in.at[pl.ds(me, 1)], req_send.at[to], req_recv.at[me], to, rep
        )

    def request_arrival(index):
        source = origin(index)
        block = req_in.at[pl.ds(source, 1)]
        return remote(block, block, req_send.at[source], req_recv.at[source], source, rep)

    def entry_copy(index):
        to = lax.rem(rep + index, peers)
        return remote(
            entry_ref, entry_in.at[pl.ds(rep, 1)], entry_send.at[to], entry_recv.at[rep], me, to
        )

    def entry_arrival(index):
        source = lax.rem(rep + peers - index, peers)
        block = entry_in.at[pl.ds(source, 1)]
        return remote(block, block, entry_send.at[source], entry_recv.at[source], me, source)

    def state_copy(index):
        to = lax.rem(rep + index, peers)
        return remote(
            send_state.at[to], carried_out.at[rep], state_send.at[to], state_recv.at[rep], me, to
        )

    def state_arrival(index):
        source = lax.rem(rep + peers - index, peers)
        block = carried_out.at[source]
        return remote(block, block, state_send.at[source], state_recv.at[source], me, source)

    def row_copy(index):
        to = partner(index)
        return remote(send_rows.at[to], rows_out.at[me], row_send.at[to], row_recv.at[me], to, rep)

    def row_arrival(index):
        source = origin(index)
        block = rows_out.at[source]
        return remote(block, block, row_send.at[source], row_recv.at[source], source, rep)

    core = lax.rem(rep, 2)
    spot = rep // 2
    other = rep + 1 - 2 * core
    spots = peers // 2
    major = my_z + core * (my_y - my_z)
    minor = my_y + core * (my_z - my_y)

    def at_plane(a, b):
        return a * (side - (side - 1) * core) + b * (1 + (side - 1) * core)

    def bundle(piece, a):
        return gathered.at[piece, pl.ds(a * side, side)]

    def near_copy(index):
        to = lax.rem(minor + index, side)
        return remote(
            pieces.at[rep],
            gathered.at[rep, major * side + minor],
            near_send.at[to],
            near_recv.at[minor],
            at_plane(major, to),
            rep,
        )

    def near_arrival(index):
        source = lax.rem(minor + side - index, side)
        block = gathered.at[rep, major * side + source]
        return remote(
            block, block, near_send.at[source], near_recv.at[source], at_plane(major, source), rep
        )

    def far_copy(index):
        to = lax.rem(major + index, side)
        return remote(
            bundle(rep, major),
            bundle(rep, major),
            far_send.at[to],
            far_recv.at[major],
            at_plane(to, minor),
            rep,
        )

    def far_arrival(index):
        source = lax.rem(major + side - index, side)
        block = bundle(rep, source)
        return remote(
            block, block, far_send.at[source], far_recv.at[source], at_plane(source, minor), rep
        )

    def line_copy(ahead, a):
        to = lax.rem(spot + ahead, spots)
        block = bundle(rep, a)
        return remote(block, block, line_send.at[to, a], line_recv.at[spot, a], me, to * 2 + core)

    def line_arrival(ahead, a):
        source = lax.rem(spot + spots - ahead, spots)
        block = bundle(source * 2 + core, a)
        return remote(
            block, block, line_send.at[source, a], line_recv.at[source, a], me, source * 2 + core
        )

    def core_copy(ahead, a):
        source = lax.rem(spot + spots - ahead, spots)
        block = bundle(source * 2 + core, a)
        return remote(block, block, core_send.at[source, a], core_recv.at[source, a], me, other)

    def core_arrival(ahead, a):
        source = lax.rem(spot + spots - ahead, spots)
        block = bundle(source * 2 + 1 - core, a)
        return remote(block, block, core_send.at[source, a], core_recv.at[source, a], me, other)

    barrier = pltpu.get_barrier_semaphore()

    @pl.loop(1, owners)
    def _(i):
        pl.semaphore_signal(barrier, inc=1, device_id=(partner(i), rep), device_id_type=MESH)

    @pl.loop(1, peers)
    def _(i):
        pl.semaphore_signal(
            barrier, inc=1, device_id=(me, lax.rem(rep + i, peers)), device_id_type=MESH
        )

    table_move = pltpu.make_async_copy(table_ref, table_here, local_sem.at[2])
    table_move.start()
    stores_move = pltpu.make_async_copy(stores_ref, stores_here, local_sem.at[3])
    stores_move.start()

    route(shard_rows, capacity, owner_ref, bag_rows_ref, req_ref, placed_out)

    half = shard_ref.shape[1]
    quarter = pieces.shape[2]
    for r in range(peers):
        lower, q = 2 * (r // 4), r % 4
        columns = slice(q * quarter, (q + 1) * quarter)
        pieces[r] = jnp.concatenate(
            [shard_ref[lower, :, columns], shard_ref[lower + 1, :, columns]], axis=0
        )

    pl.semaphore_wait(barrier, owners - 1 + peers - 1)

    @pl.loop(1, owners)
    def _(i):
        request_copy(i).start()

    @pl.loop(1, side)
    def _(i):
        near_copy(i).start()

    @pl.loop(1, peers)
    def _(i):
        entry_copy(i).start()

    req_in[pl.ds(me, 1), :] = req_ref[pl.ds(me, 1), :]
    entry_in[pl.ds(rep, 1), :] = entry_ref[...]
    gathered[rep, major * side + minor] = pieces[rep]

    tile = 256
    table_move.wait()

    @pl.loop(0, table_here.shape[0] // tile)
    def _(i):
        at = pl.multiple_of(i * tile, tile)
        wide_table[pl.ds(at, tile), :] = table_here[pl.ds(at, tile), :].astype(jnp.float32)

    @pl.loop(1, side)
    def _(i):
        near_arrival(i).wait_recv()

    @pl.loop(1, side)
    def _(i):
        far_copy(i).start()

    @pl.loop(1, owners)
    def _(i):
        request_arrival(i).wait_recv()

    req_move = pltpu.make_async_copy(req_in, req_words, local_sem.at[0])
    req_move.start()
    req_move.wait()

    def gather(to):
        for u in range(capacity):
            stage[u : u + 1, :] = wide_table[pl.ds(req_words[to, u], 1), :]
        send_rows[to] = stage[...].astype(jnp.bfloat16)

    @pl.loop(1, owners)
    def _(i):
        gather(partner(i))
        row_copy(i).start()

    @pl.loop(0, side)
    def _(i):
        a = lax.rem(major + side - i, side)

        @pl.when(i > 0)
        def _():
            far_arrival(i).wait_recv()

        for ahead in range(1, spots):
            line_copy(ahead, a).start()
        core_copy(0, a).start()

    gather(me)
    own_rows = pltpu.make_async_copy(send_rows.at[me], rows_out.at[me], local_sem.at[0])
    own_rows.start()

    stores_move.wait()
    wide_stores[...] = stores_here[...].astype(jnp.float32)
    state_stage[...] = jnp.zeros_like(state_stage)

    @pl.loop(1, peers)
    def _(i):
        entry_arrival(i).wait_recv()

    entry_move = pltpu.make_async_copy(entry_in, entry_words, local_sem.at[1])
    entry_move.start()
    entry_move.wait()

    @pl.loop(0, peers)
    def _(i):
        to = lax.rem(rep + i, peers)
        chosen = entry_words[to, 0]
        for row in range(stores_here.shape[0]):
            state_stage[row : row + 1, :] = wide_stores[row, pl.ds(chosen, 1), :]
        send_state[to] = state_stage[...].astype(jnp.bfloat16)

    @pl.loop(1, peers)
    def _(i):
        state_copy(i).start()

    own_state = pltpu.make_async_copy(send_state.at[rep], carried_out.at[rep], local_sem.at[1])
    own_state.start()

    @pl.loop(0, side)
    def _(i):
        a = lax.rem(major + side - i, side)
        for ahead in range(1, spots):
            line_arrival(ahead, a).wait_recv()
            core_copy(ahead, a).start()

    @pl.loop(0, side)
    def _(a):
        for ahead in range(spots):
            core_arrival(ahead, a).wait_recv()

    @pl.loop(0, owners // 2)
    def _(i):
        for r in range(peers):
            lower, q = 2 * (r // 4), r % 4
            columns = slice(q * quarter, (q + 1) * quarter)
            if r % 2 == 0:
                first, second = gathered[r, 2 * i], gathered[r, 2 * i + 1]
            else:
                slot = lax.rem(2 * i, side) * side + (2 * i) // side
                first, second = gathered[r, slot], gathered[r, slot + side]
            at = pl.multiple_of(i * 2 * half, 2 * half)
            filters_out[lower, pl.ds(at, 2 * half), columns] = jnp.concatenate(
                [first[:half], second[:half]], axis=0
            )
            filters_out[lower + 1, pl.ds(at, 2 * half), columns] = jnp.concatenate(
                [first[half:], second[half:]], axis=0
            )

    @pl.loop(1, side)
    def _(i):
        near_copy(i).wait_send()
        far_copy(i).wait_send()

    @pl.loop(0, side)
    def _(a):
        for ahead in range(1, spots):
            line_copy(ahead, a).wait_send()
        for ahead in range(spots):
            core_copy(ahead, a).wait_send()

    own_rows.wait()
    own_state.wait()

    @pl.loop(1, peers)
    def _(i):
        entry_copy(i).wait_send()
        state_copy(i).wait_send()
        state_arrival(i).wait_recv()

    @pl.loop(1, owners)
    def _(i):
        request_copy(i).wait_send()
        row_copy(i).wait_send()
        row_arrival(i).wait_recv()


def convolve_kernel(
    rows_ref,
    placed_ref,
    weight_ref,
    where_ref,
    carried_ref,
    filters_ref,
    gain_ref,
    out_ref,
    wide_rows,
    places,
    place_sem,
    weights_in,
    stage,
    even_in,
    odd_in,
):
    f32, bf16 = jnp.float32, jnp.bfloat16
    bag, slots = weight_ref.shape
    width = rows_ref.shape[1]
    channels = out_ref.shape[1]
    layers = filters_ref.shape[0]
    head = even_in.shape[0] - slots
    tile = 512
    moves = [
        pltpu.make_async_copy(
            placed_ref.at[k], places.at[pl.ds(k * slots, slots)], place_sem.at[k]
        )
        for k in range(bag)
    ]
    for move in moves:
        move.start()
    weights_in[...] = jnp.transpose(weight_ref[...])

    @pl.loop(0, rows_ref.shape[0] // tile)
    def _(i):
        at = pl.multiple_of(i * tile, tile)
        wide_rows[pl.ds(at, tile), :] = rows_ref[pl.ds(at, tile), :].astype(f32)

    for move in moves:
        move.wait()

    @pl.loop(0, slots // 8)
    def _(i):
        base = pl.multiple_of(i * 8, 8)
        for k in range(bag):
            for j in range(8):
                stage[k * 8 + j : k * 8 + j + 1, :] = wide_rows[
                    pl.ds(places[k * slots + base + j], 1), :
                ]
        weights = weights_in[pl.ds(base, 8), :]
        terms = [stage[k * 8 : k * 8 + 8, :] * weights[:, k : k + 1] for k in range(bag)]
        sums = (
            terms[0],
            terms[1],
            terms[2] + terms[3],
            (terms[4] + terms[5]) + (terms[6] + terms[7]),
        )
        for t in range(4):
            even_in[pl.ds(head + base, 8), t * width : (t + 1) * width] = (
                sums[t].astype(bf16).astype(f32)
            )

    state = carried_ref[where_ref[0]].astype(f32)
    state = jnp.where(where_ref[1] > 0, state, 0.0)
    block = 256
    offset = 0
    for layer in range(layers):
        dilation = 2**layer
        span = 2 * dilation
        source, target = (even_in, odd_in) if layer % 2 == 0 else (odd_in, even_in)
        source[head - span : head, :] = state[offset : offset + span, :]
        offset = offset + span
        for part in range(slots // block):
            low = head + part * block
            taps = [
                source[low - tap * dilation : low - tap * dilation + block, :].astype(bf16)
                for tap in range(3)
            ]
            values = jnp.dot(
                jnp.concatenate(taps, axis=1), filters_ref[layer], preferred_element_type=f32
            )
            mean = jnp.mean(values, axis=-1, keepdims=True)
            centred = values - mean
            spread = jnp.mean(centred * centred, axis=-1, keepdims=True)
            active = jnp.maximum(
                centred * lax.rsqrt(spread + epsilon) * gain_ref[layer : layer + 1, :], 0.0
            )
            if layer % 2 == 1:
                active = active + target[low : low + block, :]
            if layer == layers - 1:
                out_ref[part * block : (part + 1) * block, :] = active.astype(bf16)
            else:
                target[low : low + block, :] = active.astype(bf16).astype(f32)


def convolve_call(rows, placed, weights, where, carried, filters, gain):
    bf16, f32 = jnp.bfloat16, jnp.float32
    bag, slots = placed.shape
    width, channels = rows.shape[1], carried.shape[2]
    return pl.pallas_call(
        convolve_kernel,
        out_shape=jax.ShapeDtypeStruct((slots, channels), bf16),
        in_specs=[
            whole(),
            whole(),
            whole(),
            whole(pltpu.SMEM),
            whole(),
            whole(),
            whole(),
        ],
        out_specs=whole(),
        scratch_shapes=[
            pltpu.VMEM((rows.shape[0], width), f32),
            pltpu.SMEM((bag * slots,), jnp.int32),
            pltpu.SemaphoreType.DMA((bag,)),
            pltpu.VMEM((slots, bag), f32),
            pltpu.VMEM((8 * bag, width), f32),
            pltpu.VMEM((32 + slots, channels), f32),
            pltpu.VMEM((32 + slots, channels), f32),
        ],
        compiler_params=pltpu.CompilerParams(vmem_limit_bytes=48 * MIB),
        name="convolve",
    )(rows, placed, weights, where, carried, filters, gain)


def local(
    bag_rows, bag_owner, bag_weight, tables, returning, home, entry, stores, conv_weight, norm_gain
):
    i32, f32, bf16 = jnp.int32, jnp.float32, jnp.bfloat16
    owners = lax.axis_size("table")
    peers = lax.axis_size("rep")
    slots, bag = bag_rows.shape[1:]
    shard_rows, width = tables.shape[1:]
    layers, _, channels = conv_weight.shape
    capacity = min(slots, (3 * slots * bag + 2 * owners - 1) // (2 * owners))
    entries, state_len = stores.shape[:2]
    state_rows = 32

    half, quarter = conv_weight.shape[1], channels // 4
    side, spots = 8, peers // 2
    dma = pltpu.SemaphoreType.DMA
    placed, rows, carried, filters = pl.pallas_call(
        functools.partial(exchange_kernel, shard_rows, capacity),
        out_shape=(
            jax.ShapeDtypeStruct((bag, slots), i32),
            jax.ShapeDtypeStruct((owners, capacity, width), bf16),
            jax.ShapeDtypeStruct((peers, state_rows, channels), bf16),
            jax.ShapeDtypeStruct((layers, owners * half, channels), bf16),
        ),
        in_specs=[whole(), whole(), whole(), whole(pl.ANY), whole(pl.ANY), whole()],
        out_specs=(whole(), whole(pl.ANY), whole(pl.ANY), whole()),
        scratch_shapes=[
            pltpu.VMEM((4 * shard_rows, width), bf16),
            pltpu.VMEM((state_len, entries, channels), bf16),
            pltpu.VMEM((4 * shard_rows, width), f32),
            pltpu.VMEM((state_len, entries, channels), f32),
            pltpu.VMEM((state_rows, channels), f32),
            pltpu.VMEM((capacity, width), f32),
            pltpu.VMEM((owners, capacity, width), bf16),
            pltpu.VMEM((owners, 256), i32),
            pltpu.VMEM((owners, 256), i32),
            pltpu.SMEM((owners, 256), i32),
            pltpu.VMEM((peers, 128), i32),
            pltpu.SMEM((peers, 128), i32),
            pltpu.VMEM((peers, state_rows, channels), bf16),
            pltpu.VMEM((peers, 2 * half, quarter), bf16),
            pltpu.VMEM((peers, owners, 2 * half, quarter), bf16),
            dma((owners,)),
            dma((owners,)),
            dma((owners,)),
            dma((owners,)),
            dma((peers,)),
            dma((peers,)),
            dma((peers,)),
            dma((peers,)),
            dma((side,)),
            dma((side,)),
            dma((side,)),
            dma((side,)),
            dma((spots, side)),
            dma((spots, side)),
            dma((spots, side)),
            dma((spots, side)),
            dma((4,)),
        ],
        compiler_params=pltpu.CompilerParams(
            collective_id=0, has_side_effects=True, vmem_limit_bytes=48 * MIB
        ),
        name="exchange",
    )(
        bag_owner[0].T,
        bag_rows[0].T,
        jnp.broadcast_to(entry[:, None], (1, 128)),
        tables.reshape(4 * shard_rows, width),
        jnp.transpose(stores, (1, 0, 2)),
        conv_weight,
    )

    hidden = convolve_call(
        rows.reshape(owners * capacity, width),
        placed,
        bag_weight[0].T,
        jnp.concatenate([home, returning]),
        carried,
        filters,
        norm_gain,
    )
    return hidden[None]


def solution(mesh):
    in_specs = (
        P(("table", "rep"), None, None),
        P(("table", "rep"), None, None),
        P(("table", "rep"), None, None),
        P(None, "table", None),
        P(("table", "rep")),
        P(("table", "rep")),
        P(("table", "rep")),
        P(("table", "rep"), None, None),
        P(None, "table", None),
        P(),
    )
    out_specs = P(("table", "rep"), None, None)
    return jax.shard_map(local, mesh=mesh, in_specs=in_specs, out_specs=out_specs, check_vma=False)
```

```python
import functools

import jax
import jax.numpy as jnp
from jax import lax
from jax.experimental import pallas as pl
from jax.experimental.pallas import tpu as pltpu
from jax.sharding import PartitionSpec as P

table_of_id = (0, 1, 2, 2, 3, 3, 3, 3)
epsilon = 1e-05
MESH = pl.DeviceIdType.MESH
MIB = 1024 * 1024


def whole(memory=pltpu.VMEM):
    return pl.BlockSpec(memory_space=memory)


def split_index(index):
    return lax.rem(index * 27, 64)


def route(shard_rows, capacity, owner_ref, rows_ref, req_ref, placed_ref):
    bag, slots = owner_ref.shape
    owners, columns = req_ref.shape
    step = 256
    f32, bf16 = jnp.float32, jnp.bfloat16
    owner_row = lax.broadcasted_iota(jnp.int32, (owners, slots), 0)
    named = jnp.zeros((owners, slots), f32)
    for k in range(bag):
        named = named + jnp.where(owner_ref[k : k + 1, :] == owner_row, 1.0, 0.0)
    before = (
        lax.broadcasted_iota(jnp.int32, (step, step), 0)
        < lax.broadcasted_iota(jnp.int32, (step, step), 1)
    ).astype(f32).astype(bf16)
    total = jnp.zeros((owners, 1), f32)
    ranked = []
    for part in range(slots // step):
        block = named[:, part * step : (part + 1) * step]
        ranked.append(total + jnp.dot(block.astype(bf16), before, preferred_element_type=f32))
        total = total + jnp.sum(block, axis=1, keepdims=True)
    ranks = jnp.concatenate(ranked, axis=1)
    place_row = lax.broadcasted_iota(jnp.int32, (columns, slots), 0)
    requests = jnp.zeros((2 * owners, columns), f32)
    for k in range(bag):
        owner = owner_ref[k : k + 1, :]
        hit = owner == owner_row
        rank = jnp.sum(jnp.where(hit, ranks, 0.0), axis=0, keepdims=True).astype(jnp.int32)
        place = owner * capacity + rank
        placed_ref[k : k + 1, :] = jnp.clip(place, 0, owners * capacity - 1)
        value = rows_ref[k : k + 1, :] + table_of_id[k] * shard_rows
        high = jnp.where(hit, (value >> 6).astype(f32), 0.0)
        low = jnp.where(hit, (value & 63).astype(f32), 0.0)
        words = jnp.concatenate([high, low], axis=0).astype(bf16)
        marks = jnp.where(place_row == rank, 1.0, 0.0).astype(bf16)
        requests = requests + lax.dot_general(
            words, marks, (((1,), (1,)), ((), ())), preferred_element_type=f32
        )
    wanted = (requests[:owners] * 64.0 + requests[owners:]).astype(jnp.int32)
    req_ref[...] = jnp.clip(wanted, 0, 4 * shard_rows - 1)


def exchange_kernel(
    shard_rows,
    capacity,
    owner_ref,
    bag_rows_ref,
    weight_ref,
    entry_ref,
    table_ref,
    stores_ref,
    shard_ref,
    pooled_out,
    carried_out,
    filters_out,
    table_here,
    stores_here,
    wide_table,
    wide_stores,
    state_stage,
    stage,
    send_rows,
    rows_in,
    flat_rows,
    weights_in,
    placed_ref,
    places,
    place_sem,
    req_ref,
    req_in,
    req_words,
    entry_in,
    entry_words,
    send_state,
    pieces,
    gathered,
    req_send,
    req_recv,
    row_send,
    row_recv,
    entry_send,
    entry_recv,
    state_send,
    state_recv,
    near_send,
    near_recv,
    far_send,
    far_recv,
    line_send,
    line_recv,
    core_send,
    core_recv,
    local_sem,
):
    owners = req_ref.shape[0]
    peers = entry_in.shape[0]
    bag, slots = owner_ref.shape
    width = table_ref.shape[1]
    side = 8
    me = lax.axis_index("table")
    rep = lax.axis_index("rep")
    my_z, my_y = me // side, lax.rem(me, side)

    def partner(index):
        offset = split_index(index)
        return lax.rem(my_z + offset // side, side) * side + lax.rem(my_y + lax.rem(offset, side), side)

    def origin(index):
        offset = split_index(index)
        return (
            lax.rem(my_z + side - offset // side, side) * side
            + lax.rem(my_y + side - lax.rem(offset, side), side)
        )

    def remote(source, target, sender, receiver, table, line):
        return pltpu.make_async_remote_copy(
            src_ref=source,
            dst_ref=target,
            send_sem=sender,
            recv_sem=receiver,
            device_id=(table, line),
            device_id_type=MESH,
        )

    def request_copy(index):
        to = partner(index)
        return remote(
            req_ref.at[pl.ds(to, 1)], req_in.at[pl.ds(me, 1)], req_send.at[to], req_recv.at[me], to, rep
        )

    def request_arrival(index):
        source = origin(index)
        block = req_in.at[pl.ds(source, 1)]
        return remote(block, block, req_send.at[source], req_recv.at[source], source, rep)

    def entry_copy(index):
        to = lax.rem(rep + index, peers)
        return remote(
            entry_ref, entry_in.at[pl.ds(rep, 1)], entry_send.at[to], entry_recv.at[rep], me, to
        )

    def entry_arrival(index):
        source = lax.rem(rep + peers - index, peers)
        block = entry_in.at[pl.ds(source, 1)]
        return remote(block, block, entry_send.at[source], entry_recv.at[source], me, source)

    def state_copy(index):
        to = lax.rem(rep + index, peers)
        return remote(
            send_state.at[to], carried_out.at[rep], state_send.at[to], state_recv.at[rep], me, to
        )

    def state_arrival(index):
        source = lax.rem(rep + peers - index, peers)
        block = carried_out.at[source]
        return remote(block, block, state_send.at[source], state_recv.at[source], me, source)

    def row_copy(index):
        to = partner(index)
        return remote(send_rows.at[to], rows_in.at[me], row_send.at[to], row_recv.at[me], to, rep)

    def row_send_to(to):
        return remote(send_rows.at[to], rows_in.at[me], row_send.at[to], row_recv.at[me], to, rep)

    def row_arrival(index):
        source = origin(index)
        block = rows_in.at[source]
        return remote(block, block, row_send.at[source], row_recv.at[source], source, rep)

    core = lax.rem(rep, 2)
    spot = rep // 2
    other = rep + 1 - 2 * core
    spots = peers // 2
    major = my_z + core * (my_y - my_z)
    minor = my_y + core * (my_z - my_y)

    def at_plane(a, b):
        return a * (side - (side - 1) * core) + b * (1 + (side - 1) * core)

    def bundle(piece, a):
        return gathered.at[piece, pl.ds(a * side, side)]

    def near_copy(index):
        to = lax.rem(minor + index, side)
        return remote(
            pieces.at[rep],
            gathered.at[rep, major * side + minor],
            near_send.at[to],
            near_recv.at[minor],
            at_plane(major, to),
            rep,
        )

    def near_arrival(index):
        source = lax.rem(minor + side - index, side)
        block = gathered.at[rep, major * side + source]
        return remote(
            block, block, near_send.at[source], near_recv.at[source], at_plane(major, source), rep
        )

    def far_copy(index):
        to = lax.rem(major + index, side)
        return remote(
            bundle(rep, major),
            bundle(rep, major),
            far_send.at[to],
            far_recv.at[major],
            at_plane(to, minor),
            rep,
        )

    def far_arrival(index):
        source = lax.rem(major + side - index, side)
        block = bundle(rep, source)
        return remote(
            block, block, far_send.at[source], far_recv.at[source], at_plane(source, minor), rep
        )

    def line_copy(ahead, a):
        to = lax.rem(spot + ahead, spots)
        block = bundle(rep, a)
        return remote(block, block, line_send.at[to, a], line_recv.at[spot, a], me, to * 2 + core)

    def line_arrival(ahead, a):
        source = lax.rem(spot + spots - ahead, spots)
        block = bundle(source * 2 + core, a)
        return remote(
            block, block, line_send.at[source, a], line_recv.at[source, a], me, source * 2 + core
        )

    def core_copy(ahead, a):
        source = lax.rem(spot + spots - ahead, spots)
        block = bundle(source * 2 + core, a)
        return remote(block, block, core_send.at[source, a], core_recv.at[source, a], me, other)

    def core_arrival(ahead, a):
        source = lax.rem(spot + spots - ahead, spots)
        block = bundle(source * 2 + 1 - core, a)
        return remote(block, block, core_send.at[source, a], core_recv.at[source, a], me, other)

    barrier = pltpu.get_barrier_semaphore()

    @pl.loop(1, owners)
    def _(i):
        pl.semaphore_signal(barrier, inc=1, device_id=(partner(i), rep), device_id_type=MESH)

    @pl.loop(1, peers)
    def _(i):
        pl.semaphore_signal(
            barrier, inc=1, device_id=(me, lax.rem(rep + i, peers)), device_id_type=MESH
        )

    table_move = pltpu.make_async_copy(table_ref, table_here, local_sem.at[2])
    table_move.start()
    stores_move = pltpu.make_async_copy(stores_ref, stores_here, local_sem.at[3])
    stores_move.start()

    route(shard_rows, capacity, owner_ref, bag_rows_ref, req_ref, placed_ref)

    half = shard_ref.shape[1]
    quarter = pieces.shape[2]
    for r in range(peers):
        lower, q = 2 * (r // 4), r % 4
        columns = slice(q * quarter, (q + 1) * quarter)
        pieces[r] = jnp.concatenate(
            [shard_ref[lower, :, columns], shard_ref[lower + 1, :, columns]], axis=0
        )

    pl.semaphore_wait(barrier, owners - 1 + peers - 1)

    gathered[rep, major * side + minor] = pieces[rep]
    req_in[pl.ds(me, 1), :] = req_ref[pl.ds(me, 1), :]
    entry_in[pl.ds(rep, 1), :] = entry_ref[...]

    @pl.loop(1, side)
    def _(i):
        near_copy(i).start()

    @pl.loop(1, owners)
    def _(i):
        request_copy(i).start()

    @pl.loop(1, peers)
    def _(i):
        entry_copy(i).start()

    @pl.loop(1, side)
    def _(i):
        near_arrival(i).wait_recv()

    @pl.loop(1, side)
    def _(i):
        far_copy(i).start()

    tile = 256
    table_move.wait()

    @pl.loop(0, table_here.shape[0] // tile)
    def _(i):
        at = pl.multiple_of(i * tile, tile)
        wide_table[pl.ds(at, tile), :] = table_here[pl.ds(at, tile), :].astype(jnp.float32)

    @pl.loop(1, owners)
    def _(i):
        request_arrival(i).wait_recv()

    req_move = pltpu.make_async_copy(req_in, req_words, local_sem.at[0])
    req_move.start()
    req_move.wait()

    def gather(to):
        for u in range(capacity):
            stage[u : u + 1, :] = wide_table[pl.ds(req_words[to, u], 1), :]
        send_rows[to] = stage[...].astype(jnp.bfloat16)

    def pass_along(i):
        a = lax.rem(major + side - i, side)

        @pl.when(i > 0)
        def _():
            far_arrival(i).wait_recv()

        for ahead in range(1, spots):
            line_copy(ahead, a).start()
        core_copy(0, a).start()

    def pass_over(i):
        a = lax.rem(major + side - i, side)
        for ahead in range(1, spots):
            line_arrival(ahead, a).wait_recv()
            core_copy(ahead, a).start()

    def send_states():
        stores_move.wait()
        wide_stores[...] = stores_here[...].astype(jnp.float32)
        state_stage[...] = jnp.zeros_like(state_stage)

        @pl.loop(1, peers)
        def _(i):
            entry_arrival(i).wait_recv()

        entry_move = pltpu.make_async_copy(entry_in, entry_words, local_sem.at[1])
        entry_move.start()
        entry_move.wait()

        @pl.loop(0, peers)
        def _(i):
            to = lax.rem(rep + i, peers)
            chosen = entry_words[to, 0]
            for row in range(stores_here.shape[0]):
                state_stage[row : row + 1, :] = wide_stores[row, pl.ds(chosen, 1), :]
            send_state[to] = state_stage[...].astype(jnp.bfloat16)

        @pl.loop(1, peers)
        def _(i):
            state_copy(i).start()

    @pl.loop(0, owners)
    def _(i):
        group = i // 4
        turn = lax.rem(i, 4)
        long, short = group // 4 + 1, lax.rem(group, 4)
        odd, back = lax.rem(turn, 2), turn // 2
        ahead_z = (1 - 2 * back) * (long + odd * (short - long))
        ahead_y = (1 - 2 * back) * (short - odd * (short + long))
        straight = jnp.where((group == 12) & (turn == 2), 1, 0)
        ahead_z = ahead_z + side + straight * (4 - ahead_z - side)
        ahead_y = ahead_y + side + straight * (4 - ahead_y - side)

        @pl.when((group != 12) | (turn < 3))
        def _():
            to = lax.rem(my_z + ahead_z, side) * side + lax.rem(my_y + ahead_y, side)
            gather(to)
            row_send_to(to).start()

    @pl.loop(0, side)
    def _(i):
        pass_along(i)

    gather(me)
    own_rows = pltpu.make_async_copy(send_rows.at[me], rows_in.at[me], local_sem.at[0])
    own_rows.start()
    send_states()
    own_state = pltpu.make_async_copy(send_state.at[rep], carried_out.at[rep], local_sem.at[1])
    own_state.start()

    moves = [
        pltpu.make_async_copy(
            placed_ref.at[k], places.at[pl.ds(k * slots, slots)], place_sem.at[k]
        )
        for k in range(bag)
    ]
    for move in moves:
        move.start()
    weights_in[...] = jnp.transpose(weight_ref[...])
    for move in moves:
        move.wait()
    def widen(source):
        at = pl.multiple_of(source * capacity, capacity)
        flat_rows[pl.ds(at, capacity), :] = rows_in[source].astype(jnp.float32)

    own_rows.wait()
    widen(me)

    @pl.loop(0, side)
    def _(i):
        pass_over(i)

    @pl.loop(0, side)
    def _(a):
        for ahead in range(spots):
            core_arrival(ahead, a).wait_recv()

    @pl.loop(0, owners // 2)
    def _(i):
        for r in range(peers):
            lower, q = 2 * (r // 4), r % 4
            columns = slice(q * quarter, (q + 1) * quarter)
            if r % 2 == 0:
                first, second = gathered[r, 2 * i], gathered[r, 2 * i + 1]
            else:
                slot = lax.rem(2 * i, side) * side + (2 * i) // side
                first, second = gathered[r, slot], gathered[r, slot + side]
            at = pl.multiple_of(i * 2 * half, 2 * half)
            filters_out[lower, pl.ds(at, 2 * half), columns] = jnp.concatenate(
                [first[:half], second[:half]], axis=0
            )
            filters_out[lower + 1, pl.ds(at, 2 * half), columns] = jnp.concatenate(
                [first[half:], second[half:]], axis=0
            )

    @pl.loop(1, owners)
    def _(i):
        row_arrival(i).wait_recv()
        widen(origin(i))

    def pool(i):
        base = pl.multiple_of(i * 8, 8)
        for k in range(bag):
            for j in range(8):
                place = places[base + (k * slots + j)]
                stage[k * 8 + j : k * 8 + j + 1, :] = flat_rows[pl.ds(place, 1), :]
        weights = weights_in[pl.ds(base, 8), :]
        terms = [stage[k * 8 : k * 8 + 8, :] * weights[:, k : k + 1] for k in range(bag)]
        sums = (
            terms[0],
            terms[1],
            terms[2] + terms[3],
            (terms[4] + terms[5]) + (terms[6] + terms[7]),
        )
        for t in range(4):
            pooled_out[pl.ds(base, 8), t * width : (t + 1) * width] = (
                sums[t].astype(jnp.bfloat16).astype(jnp.float32)
            )

    @pl.loop(0, slots // 8)
    def _(i):
        pool(i)

    @pl.loop(1, side)
    def _(i):
        near_copy(i).wait_send()
        far_copy(i).wait_send()

    @pl.loop(0, side)
    def _(a):
        for ahead in range(1, spots):
            line_copy(ahead, a).wait_send()
        for ahead in range(spots):
            core_copy(ahead, a).wait_send()

    own_state.wait()

    @pl.loop(1, peers)
    def _(i):
        entry_copy(i).wait_send()
        state_copy(i).wait_send()
        state_arrival(i).wait_recv()

    @pl.loop(1, owners)
    def _(i):
        request_copy(i).wait_send()
        row_copy(i).wait_send()


def convolve_kernel(
    pooled_ref, where_ref, carried_ref, filters_ref, gain_ref, out_ref, even_in, odd_in
):
    f32, bf16 = jnp.float32, jnp.bfloat16
    slots = pooled_ref.shape[0]
    layers = filters_ref.shape[0]
    head = even_in.shape[0] - slots
    even_in[head:, :] = pooled_ref[...]
    state = carried_ref[where_ref[0]].astype(f32)
    state = jnp.where(where_ref[1] > 0, state, 0.0)
    block = 256
    offset = 0
    for layer in range(layers):
        dilation = 2**layer
        span = 2 * dilation
        source, target = (even_in, odd_in) if layer % 2 == 0 else (odd_in, even_in)
        source[head - span : head, :] = state[offset : offset + span, :]
        offset = offset + span
        for part in range(slots // block):
            low = head + part * block
            taps = [
                source[low - tap * dilation : low - tap * dilation + block, :].astype(bf16)
                for tap in range(3)
            ]
            values = jnp.dot(
                jnp.concatenate(taps, axis=1), filters_ref[layer], preferred_element_type=f32
            )
            mean = jnp.mean(values, axis=-1, keepdims=True)
            centred = values - mean
            spread = jnp.mean(centred * centred, axis=-1, keepdims=True)
            active = jnp.maximum(
                centred * lax.rsqrt(spread + epsilon) * gain_ref[layer : layer + 1, :], 0.0
            )
            if layer % 2 == 1:
                active = active + target[low : low + block, :]
            if layer == layers - 1:
                out_ref[part * block : (part + 1) * block, :] = active.astype(bf16)
            else:
                target[low : low + block, :] = active.astype(bf16).astype(f32)


def local(
    bag_rows, bag_owner, bag_weight, tables, returning, home, entry, stores, conv_weight, norm_gain
):
    i32, f32, bf16 = jnp.int32, jnp.float32, jnp.bfloat16
    owners = lax.axis_size("table")
    peers = lax.axis_size("rep")
    slots, bag = bag_rows.shape[1:]
    shard_rows, width = tables.shape[1:]
    layers, _, channels = conv_weight.shape
    capacity = min(slots, (3 * slots * bag + 2 * owners - 1) // (2 * owners))
    entries, state_len = stores.shape[:2]
    state_rows = 32

    half, quarter = conv_weight.shape[1], channels // 4
    side, spots = 8, peers // 2
    dma = pltpu.SemaphoreType.DMA
    pooled, carried, filters = pl.pallas_call(
        functools.partial(exchange_kernel, shard_rows, capacity),
        out_shape=(
            jax.ShapeDtypeStruct((slots, 4 * width), f32),
            jax.ShapeDtypeStruct((peers, state_rows, channels), bf16),
            jax.ShapeDtypeStruct((layers, owners * half, channels), bf16),
        ),
        in_specs=[whole(), whole(), whole(), whole(), whole(pl.ANY), whole(pl.ANY), whole()],
        out_specs=(whole(), whole(pl.ANY), whole()),
        scratch_shapes=[
            pltpu.VMEM((4 * shard_rows, width), bf16),
            pltpu.VMEM((state_len, entries, channels), bf16),
            pltpu.VMEM((4 * shard_rows, width), f32),
            pltpu.VMEM((state_len, entries, channels), f32),
            pltpu.VMEM((state_rows, channels), f32),
            pltpu.VMEM((capacity, width), f32),
            pltpu.VMEM((owners, capacity, width), bf16),
            pltpu.VMEM((owners, capacity, width), bf16),
            pltpu.VMEM((owners * capacity, width), f32),
            pltpu.VMEM((slots, bag), f32),
            pltpu.VMEM((bag, slots), i32),
            pltpu.SMEM((bag * slots,), i32),
            dma((bag,)),
            pltpu.VMEM((owners, 256), i32),
            pltpu.VMEM((owners, 256), i32),
            pltpu.SMEM((owners, 256), i32),
            pltpu.VMEM((peers, 128), i32),
            pltpu.SMEM((peers, 128), i32),
            pltpu.VMEM((peers, state_rows, channels), bf16),
            pltpu.VMEM((peers, 2 * half, quarter), bf16),
            pltpu.VMEM((peers, owners, 2 * half, quarter), bf16),
            dma((owners,)),
            dma((owners,)),
            dma((owners,)),
            dma((owners,)),
            dma((peers,)),
            dma((peers,)),
            dma((peers,)),
            dma((peers,)),
            dma((side,)),
            dma((side,)),
            dma((side,)),
            dma((side,)),
            dma((spots, side)),
            dma((spots, side)),
            dma((spots, side)),
            dma((spots, side)),
            dma((4,)),
        ],
        compiler_params=pltpu.CompilerParams(
            collective_id=0, has_side_effects=True, vmem_limit_bytes=48 * MIB
        ),
        name="exchange",
    )(
        bag_owner[0].T,
        bag_rows[0].T,
        bag_weight[0].T,
        jnp.broadcast_to(entry[:, None], (1, 128)),
        tables.reshape(4 * shard_rows, width),
        jnp.transpose(stores, (1, 0, 2)),
        conv_weight,
    )

    hidden = pl.pallas_call(
        convolve_kernel,
        out_shape=jax.ShapeDtypeStruct((slots, channels), bf16),
        in_specs=[whole(), whole(pltpu.SMEM), whole(), whole(), whole()],
        out_specs=whole(),
        scratch_shapes=[
            pltpu.VMEM((32 + slots, channels), f32),
            pltpu.VMEM((32 + slots, channels), f32),
        ],
        compiler_params=pltpu.CompilerParams(vmem_limit_bytes=40 * MIB),
        name="convolve",
    )(pooled, jnp.concatenate([home, returning]), carried, filters, norm_gain)
    return hidden[None]


def solution(mesh):
    in_specs = (
        P(("table", "rep"), None, None),
        P(("table", "rep"), None, None),
        P(("table", "rep"), None, None),
        P(None, "table", None),
        P(("table", "rep")),
        P(("table", "rep")),
        P(("table", "rep")),
        P(("table", "rep"), None, None),
        P(None, "table", None),
        P(),
    )
    out_specs = P(("table", "rep"), None, None)
    return jax.shard_map(local, mesh=mesh, in_specs=in_specs, out_specs=out_specs, check_vma=False)
```
